32 devices in a mesh: dp: 8 (over z, x), mp: 4 (over y, core).
Axes of the slice: x: 2, y: 2, z: 4, core: 2. Of those that a mesh axis runs over, the one named last changes fastest.
Arguments:
- features: bfloat16 [4096, 4096], P('dp', 'mp'), may hold values from -12 to 12
- out_grad: bfloat16 [4096, 14336], P('dp', 'mp'), may hold values from -0.09375 to 0.09375
- sketch: float32 [14336, 256], P('mp'), may hold values from -0.046875 to 0.046875
Outputs:
- projector: float32 [4096, 256], P('mp')
- projected: float32 [256, 14336], P('dp', 'mp')
The draws below stay inside these ranges and needn't reach their ends.
All inputs are finite; a program needn't handle non-finite values.
Results may differ from the reference program's by a relative error of at most 0.00055.
Values sent between devices are 32-bit elements; how exact they have to be, the bound alone decides.
A program may use at most 64 MiB of HBM per device.

```python
import jax
import jax.numpy as jnp
from jax import lax

M = 4096
FF = 14336
R = 256
TOKENS = 4096


def draw_features(key, part):
    key = jax.random.fold_in(key, 11)
    order_key, noise_key = jax.random.split(key, 2)
    ranks = jax.random.permutation(order_key, M).astype(jnp.float32) + 1.0
    column_scale = 3.0 * ranks ** (-0.75)
    noise = jax.random.truncated_normal(noise_key, -4.0, 4.0, (TOKENS, M), jnp.float32)
    values = noise * column_scale[None, :]
    return values.astype(jnp.bfloat16)


def steps_of(rng, shape, cuts, least, largest):
    def one(dim, parts):
        steps = jax.random.uniform(jax.random.fold_in(jax.random.fold_in(rng, 6), dim), (parts,), jnp.float32, least / len(cuts), largest / len(cuts))
        return jnp.repeat(jnp.exp(steps), shape[dim] // parts).reshape((-1,) + (1,) * (len(shape) - dim - 1))

    gain = one(*cuts[0])
    for cut in cuts[1:]:
        gain = gain * one(*cut)
    return gain


def bell_draw(own_key, dims, spread, limit, pieces=(), dtype=jnp.bfloat16):
    values = spread * jax.random.normal(own_key, dims, jnp.float32)
    if pieces:
        values = values * steps_of(own_key, dims, pieces, -0.22, 0.18)
    return jnp.clip(values, -limit, limit).astype(dtype)


def setup_inputs(seed: int = 0) -> dict:
    streams_of = jax.random.split(jax.random.key(seed), 4)
    features = draw_features(jax.random.fold_in(streams_of[3], 71), 0)
    out_grad = bell_draw(streams_of[1], (TOKENS, FF), (TOKENS ** -0.5), 0.09375, ((0, 8), (1, 4)))
    sketch = bell_draw(streams_of[2], (FF, R), FF ** -0.5, 0.046875, ((0, 4),), jnp.float32)
    return dict(features=features, out_grad=out_grad, sketch=sketch)


def orth(panel):
    highest = lax.Precision.HIGHEST
    gram_sum = jnp.dot(panel.T.astype(jnp.float32), panel.astype(jnp.float32), precision=highest, preferred_element_type=jnp.float32)
    factor = jnp.linalg.cholesky(gram_sum)
    return lax.linalg.triangular_solve(factor, panel, left_side=False, lower=True, transpose_a=True)

def reference(features, out_grad, sketch):
    highest = lax.Precision.HIGHEST
    sketched = jnp.dot(out_grad.astype(jnp.float32), sketch.astype(jnp.float32), precision=highest, preferred_element_type=jnp.float32)
    panel_one = jnp.einsum('tm,tr->mr', features.astype(jnp.float32), sketched.astype(jnp.float32), precision=highest, preferred_element_type=jnp.float32)
    basis = orth(panel_one)
    image = jnp.dot(features.astype(jnp.float32), basis.astype(jnp.float32), precision=highest, preferred_element_type=jnp.float32)
    wide = jnp.einsum('tf,tr->fr', out_grad.astype(jnp.float32), image.astype(jnp.float32), precision=highest, preferred_element_type=jnp.float32)
    second = jnp.dot(out_grad.astype(jnp.float32), wide.astype(jnp.float32), precision=highest, preferred_element_type=jnp.float32)
    panel_two = jnp.einsum('tm,tr->mr', features.astype(jnp.float32), second.astype(jnp.float32), precision=highest, preferred_element_type=jnp.float32)
    projector = orth(orth(panel_two))
    mapped = jnp.dot(features.astype(jnp.float32), projector.astype(jnp.float32), precision=highest, preferred_element_type=jnp.float32)
    projected = jnp.einsum('tr,tf->rf', mapped.astype(jnp.float32), out_grad.astype(jnp.float32), precision=highest, preferred_element_type=jnp.float32)
    return (projector, projected)
```

```python
import functools

import jax
import jax.numpy as jnp
from jax import lax
from jax.experimental import pallas as pl
from jax.experimental.pallas import tpu as pltpu
from jax.sharding import PartitionSpec as P

F32 = jnp.float32
HIGHEST = lax.Precision.HIGHEST
VMEM = pl.BlockSpec(memory_space=pltpu.VMEM)
BLOCK = 128


def sum_kernel(axis, n, gather, x_ref, out_ref, near, total, far, sems):
    groups = n // 2
    me = lax.axis_index(axis)
    parity = lax.rem(me, 2)
    group = lax.div(me, 2)
    mate = me + 1 - 2 * parity

    def member(k):
        return lax.rem(group + k, groups)

    def send(src, dst, row, slot, target):
        copy = pltpu.make_async_remote_copy(
            src_ref=src,
            dst_ref=dst,
            send_sem=sems.at[2 * row, slot],
            recv_sem=sems.at[2 * row + 1, slot],
            device_id={axis: target},
            device_id_type=pl.DeviceIdType.MESH,
        )
        copy.start()
        return copy

    barrier = pltpu.get_barrier_semaphore()
    pl.semaphore_signal(barrier, inc=1, device_id={axis: mate}, device_id_type=pl.DeviceIdType.MESH)
    for k in range(1, groups):
        pl.semaphore_signal(
            barrier, inc=1, device_id={axis: 2 * member(k) + parity}, device_id_type=pl.DeviceIdType.MESH
        )
    pl.semaphore_wait(barrier, groups)

    order = list(range(1, groups)) + [0]
    first = {k: send(x_ref.at[2 * member(k) + 1 - parity], near.at[k], 0, k, mate) for k in order}
    second = {}
    for k in order:
        first[k].wait_recv()
        total[k] = x_ref[2 * member(k) + parity] + near[k]
        if k:
            second[k] = send(total.at[k], far.at[k - 1], 1, k, 2 * member(k) + parity)
    mine = total[0]
    for k in range(1, groups):
        second[k].wait_recv()
        mine = mine + far[k - 1]
    copies = list(first.values()) + list(second.values())
    waits = []
    if gather:
        out_ref[me] = mine
        across = [send(out_ref.at[me], out_ref.at[me], 2, k, 2 * member(k) + parity) for k in range(1, groups)]
        side = [send(out_ref.at[me], out_ref.at[me], 3, 0, mate)]
        for k in range(1, groups):
            across[k - 1].wait_recv()
            block = out_ref.at[2 * member(groups - k) + parity]
            side.append(send(block, block, 3, k, mate))
        for copy in side:
            copy.wait_recv()
        copies += across + side
    else:
        out_ref[...] = mine
    for copy in copies:
        copy.wait_send()


def summed(x, axis, n, ident, gather=True):
    rows, columns = x.shape
    piece = rows // n
    groups = n // 2
    size = 4 * rows * columns
    out = pl.pallas_call(
        functools.partial(sum_kernel, axis, n, gather),
        out_shape=jax.ShapeDtypeStruct((n, piece, columns) if gather else (piece, columns), F32),
        in_specs=[VMEM],
        out_specs=VMEM,
        scratch_shapes=[
            pltpu.VMEM((groups, piece, columns), F32),
            pltpu.VMEM((groups, piece, columns), F32),
            pltpu.VMEM((max(groups - 1, 1), piece, columns), F32),
            pltpu.SemaphoreType.DMA((8, groups)),
        ],
        compiler_params=pltpu.CompilerParams(
            collective_id=ident, has_side_effects=True, vmem_limit_bytes=6 * size + (8 << 20)
        ),
    )(x.reshape(n, piece, columns))
    return out.reshape(rows, columns) if gather else out


def inverse_factor(a):
    tiles = BLOCK // 8
    sub = lax.broadcasted_iota(jnp.int32, (8, 1), 0)
    lane = lax.broadcasted_iota(jnp.int32, (8, BLOCK), 1)
    eye_row = lax.broadcasted_iota(jnp.int32, (8, BLOCK), 0)
    left = [a[8 * i : 8 * i + 8, :] for i in range(tiles)]
    right = [jnp.where(lane == eye_row + 8 * i, 1.0, 0.0).astype(F32) for i in range(tiles)]
    pivots = [jnp.ones((8, 1), F32) for _ in range(tiles)]
    for j in range(BLOCK):
        t, s = j // 8, j % 8
        row = left[t][s : s + 1, :]
        pivot = row[:, j : j + 1]
        scale = 1.0 / pivot
        pivots[t] = jnp.where(sub == s, pivot, pivots[t])
        row = row * scale
        other = right[t][s : s + 1, :] * scale
        for i in range(t, tiles):
            if i == t and s == 7:
                continue
            col = left[i][:, j : j + 1]
            if i == t:
                col = jnp.where(sub > s, col, 0.0)
            left[i] = left[i] - col * row
            right[i] = right[i] - col * other
    return jnp.concatenate([right[i] * (1.0 / jnp.sqrt(pivots[i])) for i in range(tiles)], axis=0)


def dot(a, b, dims=((1,), (0,))):
    return lax.dot_general(a, b, (dims, ((), ())), precision=HIGHEST, preferred_element_type=F32)


def solve_kernel(count, gram_ref, *refs):
    inv, low, rest = refs[-3:]
    blocks = gram_ref.shape[0] // BLOCK
    rest[...] = gram_ref[...]
    inv[...] = jnp.zeros_like(inv)

    @pl.loop(0, blocks)
    def _(b):
        at = pl.ds(pl.multiple_of(b * BLOCK, BLOCK), BLOCK)
        w = inverse_factor(rest[at, at])
        low[...] = dot(rest[:, at], w, ((1,), (1,)))
        rest[...] = rest[...] - dot(low[...], low[...], ((1,), (1,)))
        inv[at, at] = w

    gram = gram_ref[...]
    for i in range(1, blocks):
        here = slice(i * BLOCK, (i + 1) * BLOCK)
        done = inv[0 : i * BLOCK, 0 : i * BLOCK]
        w = inv[here, here]
        factor = dot(gram[here, 0 : i * BLOCK], done, ((1,), (1,)))
        inv[here, 0 : i * BLOCK] = -dot(w, dot(factor, done))
    for index in range(count):
        refs[count + index][...] = dot(refs[index][...], inv[...], ((1,), (1,)))


def solved(gram, *panels):
    rank = gram.shape[0]
    return pl.pallas_call(
        functools.partial(solve_kernel, len(panels)),
        out_shape=[jax.ShapeDtypeStruct(p.shape, F32) for p in panels],
        in_specs=[VMEM] * (1 + len(panels)),
        out_specs=[VMEM] * len(panels),
        scratch_shapes=[
            pltpu.VMEM((rank, rank), F32),
            pltpu.VMEM((rank, BLOCK), F32),
            pltpu.VMEM((rank, rank), F32),
        ],
        compiler_params=pltpu.CompilerParams(vmem_limit_bytes=32 << 20),
    )(gram, *panels)


def pieces(value):
    terms = []
    for _ in range(3):
        term = lax.reduce_precision(value, 8, 7)
        terms.append(term.astype(jnp.bfloat16))
        value = value - term
    return terms


def exact_dot(a, b, contract):
    width = b.shape[1]
    c = lax.dot_general(
        a,
        jnp.concatenate(pieces(b), axis=1),
        (((contract,), (0,)), ((), ())),
        preferred_element_type=F32,
    )
    return c[:, :width] + (c[:, width : 2 * width] + c[:, 2 * width :])


def per_device(dp, mp, features, out_grad, sketch):
    tokens = features.shape[0]
    rank = sketch.shape[1]
    sketched = summed(exact_dot(out_grad, sketch, 1), "mp", mp, 0)
    panel = summed(exact_dot(features, sketched, 0), "dp", dp, 1)
    both = summed(
        jnp.concatenate([exact_dot(features, panel, 1), dot(panel, panel, ((0,), (0,)))]), "mp", mp, 2
    )
    (image,) = solved(both[tokens:], both[:tokens])
    wide = summed(exact_dot(out_grad, image, 0), "dp", dp, 3)
    second = summed(exact_dot(out_grad, wide, 1), "mp", mp, 4)
    panel = summed(exact_dot(features, second, 0), "dp", dp, 5)
    (panel,) = solved(summed(dot(panel, panel, ((0,), (0,))), "mp", mp, 6), panel)
    both = summed(
        jnp.concatenate([exact_dot(features, panel, 1), dot(panel, panel, ((0,), (0,)))]), "mp", mp, 7
    )
    projector, mapped = solved(both[tokens:], panel, both[:tokens])
    terms = jnp.concatenate(pieces(mapped), axis=1)
    c = lax.dot_general(terms, out_grad, (((0,), (0,)), ((), ())), preferred_element_type=F32)
    share = c[:rank] + (c[rank : 2 * rank] + c[2 * rank :])
    return (projector, summed(share, "dp", dp, 8, gather=False))


def solution(mesh):
    return jax.shard_map(
        functools.partial(per_device, mesh.shape["dp"], mesh.shape["mp"]),
        mesh=mesh,
        in_specs=(P("dp", "mp"), P("dp", "mp"), P("mp", None)),
        out_specs=(P("mp", None), P("dp", "mp")),
        check_vma=False,
    )
```

```python
import functools

import jax
import jax.numpy as jnp
from jax import lax
from jax.experimental import pallas as pl
from jax.experimental.pallas import tpu as pltpu
from jax.sharding import PartitionSpec as P

F32 = jnp.float32
HIGHEST = lax.Precision.HIGHEST
VMEM = pl.BlockSpec(memory_space=pltpu.VMEM)
BLOCK = 128
WIDTH = 4


def sum_kernel(axis, n, parts, gather, x_ref, out_ref, near, total, far, sems):
    groups = n // 2
    me = lax.axis_index(axis)
    parity = lax.rem(me, 2)
    group = lax.div(me, 2)
    mate = me + 1 - 2 * parity

    def member(k):
        return lax.rem(group + k, groups)

    def send(src, dst, row, slot, target):
        copy = pltpu.make_async_remote_copy(
            src_ref=src,
            dst_ref=dst,
            send_sem=sems.at[2 * row, slot],
            recv_sem=sems.at[2 * row + 1, slot],
            device_id={axis: target},
            device_id_type=pl.DeviceIdType.MESH,
        )
        copy.start()
        return copy

    barrier = pltpu.get_barrier_semaphore()
    pl.semaphore_signal(barrier, inc=1, device_id={axis: mate}, device_id_type=pl.DeviceIdType.MESH)
    for k in range(1, groups):
        pl.semaphore_signal(
            barrier, inc=1, device_id={axis: 2 * member(k) + parity}, device_id_type=pl.DeviceIdType.MESH
        )
    pl.semaphore_wait(barrier, groups)

    order = list(range(1, groups)) + [0]
    first, second, across, side = {}, {}, {}, {}
    for s in range(parts):
        for k in order:
            first[k, s] = send(
                x_ref.at[2 * member(k) + 1 - parity, s], near.at[k, s], 0, k * parts + s, mate
            )

    def pair(s):
        for k in order:
            first[k, s].wait_recv()
            total[k, s] = x_ref[2 * member(k) + parity, s] + near[k, s]
            if k:
                second[k, s] = send(
                    total.at[k, s], far.at[k - 1, s], 1, k * parts + s, 2 * member(k) + parity
                )

    def finish(s):
        mine = total[0, s]
        for k in range(1, groups):
            second[k, s].wait_recv()
            mine = mine + far[k - 1, s]
        if not gather:
            out_ref[s] = mine
            return
        out_ref[me, s] = mine
        block = out_ref.at[me, s]
        for k in range(1, groups):
            across[k, s] = send(block, block, 2, k * parts + s, 2 * member(k) + parity)
        side[0, s] = send(block, block, 3, s, mate)

    def forward(s):
        for k in range(1, groups):
            across[k, s].wait_recv()
            block = out_ref.at[2 * member(groups - k) + parity, s]
            side[k, s] = send(block, block, 3, k * parts + s, mate)

    for turn in range(parts + 2):
        if turn < parts:
            pair(turn)
        if 0 <= turn - 1 < parts:
            finish(turn - 1)
        if gather and 0 <= turn - 2:
            forward(turn - 2)
    for copy in side.values():
        copy.wait_recv()
    for copies in (first, second, across, side):
        for copy in copies.values():
            copy.wait_send()


def summed(x, axis, n, ident, gather=True, parts=1):
    rows, columns = x.shape
    while parts > 1 and rows % (8 * n * parts):
        parts -= 1
    piece = (parts, rows // n // parts, columns)
    groups = n // 2
    size = 4 * rows * columns
    out = pl.pallas_call(
        functools.partial(sum_kernel, axis, n, parts, gather),
        out_shape=jax.ShapeDtypeStruct((n, *piece) if gather else piece, F32),
        in_specs=[VMEM],
        out_specs=VMEM,
        scratch_shapes=[
            pltpu.VMEM((groups, *piece), F32),
            pltpu.VMEM((groups, *piece), F32),
            pltpu.VMEM((max(groups - 1, 1), *piece), F32),
            pltpu.SemaphoreType.DMA((8, groups * parts)),
        ],
        compiler_params=pltpu.CompilerParams(
            collective_id=ident, has_side_effects=True, vmem_limit_bytes=6 * size + (8 << 20)
        ),
    )(x.reshape(n, *piece))
    return out.reshape(rows if gather else rows // n, columns)


def inverse_factor(a):
    tiles = BLOCK // 8
    sub = lax.broadcasted_iota(jnp.int32, (8, BLOCK), 0)
    lane = lax.broadcasted_iota(jnp.int32, (8, BLOCK), 1)
    left = [a[8 * i : 8 * i + 8, :] for i in range(tiles)]
    right = [jnp.where(lane == sub + 8 * i, 1.0, 0.0).astype(F32) for i in range(tiles)]
    pivots = [jnp.ones((8, BLOCK), F32) for _ in range(tiles)]
    for start in range(0, BLOCK, WIDTH):
        t = start // 8
        cols = {
            i: [jnp.broadcast_to(left[i][:, start + m : start + m + 1], (8, BLOCK)) for m in range(WIDTH)]
            for i in range(t, tiles)
        }
        for k in range(WIDTH):
            s = (start + k) % 8
            pivot = cols[t][k][s : s + 1, :]
            scale = 1.0 / pivot
            pivots[t] = jnp.where(sub == s, pivot, pivots[t])
            row = left[t][s : s + 1, :] * scale
            other = right[t][s : s + 1, :] * scale
            heads = {m: cols[t][m][s : s + 1, :] * scale for m in range(k + 1, WIDTH)}
            for i in range(t, tiles):
                if i == t and s == 7:
                    continue
                col = cols[i][k]
                if i == t:
                    col = jnp.where(sub > s, col, 0.0)
                left[i] = left[i] - col * row
                right[i] = right[i] - col * other
                for m in heads:
                    cols[i][m] = cols[i][m] - col * heads[m]
    return jnp.concatenate([right[i] * (1.0 / jnp.sqrt(pivots[i])) for i in range(tiles)], axis=0)


def dot(a, b, dims=((1,), (0,))):
    return lax.dot_general(a, b, (dims, ((), ())), precision=HIGHEST, preferred_element_type=F32)


def solve_kernel(count, gram_ref, *refs):
    inv, low, rest = refs[-3:]
    blocks = gram_ref.shape[0] // BLOCK
    rest[...] = gram_ref[...]
    inv[...] = jnp.zeros_like(inv)

    @pl.loop(0, blocks)
    def _(b):
        at = pl.ds(pl.multiple_of(b * BLOCK, BLOCK), BLOCK)
        w = inverse_factor(rest[at, at])
        low[...] = dot(rest[:, at], w, ((1,), (1,)))
        rest[...] = rest[...] - dot(low[...], low[...], ((1,), (1,)))
        inv[at, at] = w

    gram = gram_ref[...]
    for i in range(1, blocks):
        here = slice(i * BLOCK, (i + 1) * BLOCK)
        done = inv[0 : i * BLOCK, 0 : i * BLOCK]
        w = inv[here, here]
        factor = dot(gram[here, 0 : i * BLOCK], done, ((1,), (1,)))
        inv[here, 0 : i * BLOCK] = -dot(w, dot(factor, done))
    for index in range(count):
        refs[count + index][...] = dot(refs[index][...], inv[...], ((1,), (1,)))


def solved(gram, *panels):
    rank = gram.shape[0]
    return pl.pallas_call(
        functools.partial(solve_kernel, len(panels)),
        out_shape=[jax.ShapeDtypeStruct(p.shape, F32) for p in panels],
        in_specs=[VMEM] * (1 + len(panels)),
        out_specs=[VMEM] * len(panels),
        scratch_shapes=[
            pltpu.VMEM((rank, rank), F32),
            pltpu.VMEM((rank, BLOCK), F32),
            pltpu.VMEM((rank, rank), F32),
        ],
        compiler_params=pltpu.CompilerParams(vmem_limit_bytes=32 << 20),
    )(gram, *panels)


def pieces(value):
    terms = []
    for _ in range(3):
        term = lax.reduce_precision(value, 8, 7)
        terms.append(term.astype(jnp.bfloat16))
        value = value - term
    return terms


def exact_dot(a, b, contract):
    width = b.shape[1]
    c = lax.dot_general(
        a,
        jnp.concatenate(pieces(b), axis=1),
        (((contract,), (0,)), ((), ())),
        preferred_element_type=F32,
    )
    return c[:, :width] + (c[:, width : 2 * width] + c[:, 2 * width :])


def exact_dot_left(b, a):
    width = b.shape[1]
    terms = jnp.concatenate(pieces(b), axis=1)
    c = lax.dot_general(terms, a, (((0,), (0,)), ((), ())), preferred_element_type=F32)
    return c[:width] + (c[width : 2 * width] + c[2 * width :])


def per_device(dp, mp, features, out_grad, sketch):
    tokens = features.shape[0]
    rank = sketch.shape[1]
    sketched = summed(exact_dot(out_grad, sketch, 1), "mp", mp, 0)
    panel = summed(exact_dot(features, sketched, 0), "dp", dp, 1, parts=2)
    both = summed(
        jnp.concatenate([exact_dot(features, panel, 1), dot(panel, panel, ((0,), (0,)))]), "mp", mp, 2
    )
    (image,) = solved(both[tokens:], both[:tokens])
    wide = summed(exact_dot_left(image, out_grad), "dp", dp, 3, parts=4)
    terms = jnp.concatenate(pieces(wide), axis=0)
    c = lax.dot_general(out_grad, terms, (((1,), (1,)), ((), ())), preferred_element_type=F32)
    second = summed(c[:, :rank] + (c[:, rank : 2 * rank] + c[:, 2 * rank :]), "mp", mp, 4)
    panel = summed(exact_dot(features, second, 0), "dp", dp, 5, parts=2)
    (panel,) = solved(summed(dot(panel, panel, ((0,), (0,))), "mp", mp, 6), panel)
    both = summed(
        jnp.concatenate([exact_dot(features, panel, 1), dot(panel, panel, ((0,), (0,)))]), "mp", mp, 7
    )
    projector, mapped = solved(both[tokens:], panel, both[:tokens])
    share = exact_dot_left(mapped, out_grad)
    return (projector, summed(share, "dp", dp, 8, gather=False, parts=2))


def solution(mesh):
    return jax.shard_map(
        functools.partial(per_device, mesh.shape["dp"], mesh.shape["mp"]),
        mesh=mesh,
        in_specs=(P("dp", "mp"), P("dp", "mp"), P("mp", None)),
        out_specs=(P("mp", None), P("dp", "mp")),
        check_vma=False,
    )
```

```python
import functools

import jax
import jax.numpy as jnp
from jax import lax
from jax.experimental import pallas as pl
from jax.experimental.pallas import tpu as pltpu
from jax.sharding import PartitionSpec as P

F32 = jnp.float32
HIGHEST = lax.Precision.HIGHEST
VMEM = pl.BlockSpec(memory_space=pltpu.VMEM)
BLOCK = 128
WIDTH = 8


def sum_kernel(axis, n, parts, gather, x_ref, out_ref, near, total, far, sems):
    groups = n // 2
    me = lax.axis_index(axis)
    parity = lax.rem(me, 2)
    group = lax.div(me, 2)
    mate = me + 1 - 2 * parity

    def member(k):
        return lax.rem(group + k, groups)

    def send(src, dst, row, slot, target):
        copy = pltpu.make_async_remote_copy(
            src_ref=src,
            dst_ref=dst,
            send_sem=sems.at[2 * row, slot],
            recv_sem=sems.at[2 * row + 1, slot],
            device_id={axis: target},
            device_id_type=pl.DeviceIdType.MESH,
        )
        copy.start()
        return copy

    barrier = pltpu.get_barrier_semaphore()
    pl.semaphore_signal(barrier, inc=1, device_id={axis: mate}, device_id_type=pl.DeviceIdType.MESH)
    for k in range(1, groups):
        pl.semaphore_signal(
            barrier, inc=1, device_id={axis: 2 * member(k) + parity}, device_id_type=pl.DeviceIdType.MESH
        )
    pl.semaphore_wait(barrier, groups)

    order = list(range(1, groups)) + [0]
    first, second, across, side = {}, {}, {}, {}
    for s in range(parts):
        for k in order:
            first[k, s] = send(
                x_ref.at[2 * member(k) + 1 - parity, s], near.at[k, s], 0, k * parts + s, mate
            )

    def pair(s):
        for k in order:
            first[k, s].wait_recv()
            total[k, s] = x_ref[2 * member(k) + parity, s] + near[k, s]
            if k:
                second[k, s] = send(
                    total.at[k, s], far.at[k - 1, s], 1, k * parts + s, 2 * member(k) + parity
                )

    def finish(s):
        mine = total[0, s]
        for k in range(1, groups):
            second[k, s].wait_recv()
            mine = mine + far[k - 1, s]
        if not gather:
            out_ref[s] = mine
            return
        out_ref[me, s] = mine
        block = out_ref.at[me, s]
        for k in range(1, groups):
            across[k, s] = send(block, block, 2, k * parts + s, 2 * member(k) + parity)
        side[0, s] = send(block, block, 3, s, mate)

    def forward(s):
        for k in range(1, groups):
            across[k, s].wait_recv()
            block = out_ref.at[2 * member(groups - k) + parity, s]
            side[k, s] = send(block, block, 3, k * parts + s, mate)

    for turn in range(parts + 2):
        if turn < parts:
            pair(turn)
        if 0 <= turn - 1 < parts:
            finish(turn - 1)
        if gather and 0 <= turn - 2:
            forward(turn - 2)
    for copy in side.values():
        copy.wait_recv()
    for copies in (first, second, across, side):
        for copy in copies.values():
            copy.wait_send()


def summed(x, axis, n, ident, gather=True, parts=1):
    rows, columns = x.shape
    while parts > 1 and rows % (8 * n * parts):
        parts -= 1
    piece = (parts, rows // n // parts, columns)
    groups = n // 2
    size = 4 * rows * columns
    out = pl.pallas_call(
        functools.partial(sum_kernel, axis, n, parts, gather),
        out_shape=jax.ShapeDtypeStruct((n, *piece) if gather else piece, F32),
        in_specs=[VMEM],
        out_specs=VMEM,
        scratch_shapes=[
            pltpu.VMEM((groups, *piece), F32),
            pltpu.VMEM((groups, *piece), F32),
            pltpu.VMEM((max(groups - 1, 1), *piece), F32),
            pltpu.SemaphoreType.DMA((8, groups * parts)),
        ],
        compiler_params=pltpu.CompilerParams(
            collective_id=ident, has_side_effects=True, vmem_limit_bytes=6 * size + (8 << 20)
        ),
    )(x.reshape(n, *piece))
    return out.reshape(rows if gather else rows // n, columns)


def inverse_factor(a):
    tiles = BLOCK // 8
    sub = lax.broadcasted_iota(jnp.int32, (8, BLOCK), 0)
    lane = lax.broadcasted_iota(jnp.int32, (8, BLOCK), 1)
    left = [a[8 * i : 8 * i + 8, :] for i in range(tiles)]
    right = [jnp.where(lane == sub + 8 * i, 1.0, 0.0).astype(F32) for i in range(tiles)]
    pivots = [jnp.ones((8, BLOCK), F32) for _ in range(tiles)]
    for start in range(0, BLOCK, WIDTH):
        t = start // 8
        cols = {
            i: [jnp.broadcast_to(left[i][:, start + m : start + m + 1], (8, BLOCK)) for m in range(WIDTH)]
            for i in range(t, tiles)
        }
        for k in range(WIDTH):
            s = (start + k) % 8
            pivot = cols[t][k][s : s + 1, :]
            scale = 1.0 / pivot
            pivots[t] = jnp.where(sub == s, pivot, pivots[t])
            row = left[t][s : s + 1, :] * scale
            other = right[t][s : s + 1, :] * scale
            heads = {m: cols[t][m][s : s + 1, :] * scale for m in range(k + 1, WIDTH)}
            for i in range(t, tiles):
                if i == t and s == 7:
                    continue
                col = cols[i][k]
                if i == t:
                    col = jnp.where(sub > s, col, 0.0)
                left[i] = left[i] - col * row
                right[i] = right[i] - col * other
                for m in heads:
                    cols[i][m] = cols[i][m] - col * heads[m]
    return jnp.concatenate([right[i] * (1.0 / jnp.sqrt(pivots[i])) for i in range(tiles)], axis=0)


def dot(a, b, dims=((1,), (0,))):
    return lax.dot_general(a, b, (dims, ((), ())), precision=HIGHEST, preferred_element_type=F32)


def solve_kernel(count, gram_ref, *refs):
    inv, low, rest = refs[-3:]
    blocks = gram_ref.shape[0] // BLOCK
    rest[...] = gram_ref[...]
    inv[...] = jnp.zeros_like(inv)

    @pl.loop(0, blocks)
    def _(b):
        at = pl.ds(pl.multiple_of(b * BLOCK, BLOCK), BLOCK)
        w = inverse_factor(rest[at, at])
        low[...] = dot(rest[:, at], w, ((1,), (1,)))
        rest[...] = rest[...] - dot(low[...], low[...], ((1,), (1,)))
        inv[at, at] = w

    gram = gram_ref[...]
    for i in range(1, blocks):
        here = slice(i * BLOCK, (i + 1) * BLOCK)
        done = inv[0 : i * BLOCK, 0 : i * BLOCK]
        w = inv[here, here]
        factor = dot(gram[here, 0 : i * BLOCK], done, ((1,), (1,)))
        inv[here, 0 : i * BLOCK] = -dot(w, dot(factor, done))
    for index in range(count):
        refs[count + index][...] = dot(refs[index][...], inv[...], ((1,), (1,)))


def solved(gram, *panels):
    rank = gram.shape[0]
    return pl.pallas_call(
        functools.partial(solve_kernel, len(panels)),
        out_shape=[jax.ShapeDtypeStruct(p.shape, F32) for p in panels],
        in_specs=[VMEM] * (1 + len(panels)),
        out_specs=[VMEM] * len(panels),
        scratch_shapes=[
            pltpu.VMEM((rank, rank), F32),
            pltpu.VMEM((rank, BLOCK), F32),
            pltpu.VMEM((rank, rank), F32),
        ],
        compiler_params=pltpu.CompilerParams(vmem_limit_bytes=32 << 20),
    )(gram, *panels)


def pieces(value):
    terms = []
    for _ in range(3):
        term = lax.reduce_precision(value, 8, 7)
        terms.append(term.astype(jnp.bfloat16))
        value = value - term
    return terms


def exact_dot(a, b, contract):
    width = b.shape[1]
    c = lax.dot_general(
        a,
        jnp.concatenate(pieces(b), axis=1),
        (((contract,), (0,)), ((), ())),
        preferred_element_type=F32,
    )
    return c[:, :width] + (c[:, width : 2 * width] + c[:, 2 * width :])


def exact_dot_left(b, a):
    width = b.shape[1]
    terms = jnp.concatenate(pieces(b), axis=1)
    c = lax.dot_general(terms, a, (((0,), (0,)), ((), ())), preferred_element_type=F32)
    return c[:width] + (c[width : 2 * width] + c[2 * width :])


def per_device(dp, mp, features, out_grad, sketch):
    tokens = features.shape[0]
    rank = sketch.shape[1]
    sketched = summed(exact_dot(out_grad, sketch, 1), "mp", mp, 0, parts=2)
    panel = summed(exact_dot(features, sketched, 0), "dp", dp, 1, parts=4)
    both = summed(
        jnp.concatenate([exact_dot(features, panel, 1), dot(panel, panel, ((0,), (0,)))]), "mp", mp, 2
    )
    (image,) = solved(both[tokens:], both[:tokens])
    wide = summed(exact_dot_left(image, out_grad), "dp", dp, 3, parts=4)
    terms = jnp.concatenate(pieces(wide), axis=0)
    c = lax.dot_general(out_grad, terms, (((1,), (1,)), ((), ())), preferred_element_type=F32)
    second = summed(c[:, :rank] + (c[:, rank : 2 * rank] + c[:, 2 * rank :]), "mp", mp, 4, parts=2)
    panel = summed(exact_dot(features, second, 0), "dp", dp, 5, parts=4)
    (panel,) = solved(summed(dot(panel, panel, ((0,), (0,))), "mp", mp, 6, parts=2), panel)
    both = summed(
        jnp.concatenate([exact_dot(features, panel, 1), dot(panel, panel, ((0,), (0,)))]), "mp", mp, 7
    )
    projector, mapped = solved(both[tokens:], panel, both[:tokens])
    share = exact_dot_left(mapped, out_grad)
    return (projector, summed(share, "dp", dp, 8, gather=False, parts=4))


def solution(mesh):
    return jax.shard_map(
        functools.partial(per_device, mesh.shape["dp"], mesh.shape["mp"]),
        mesh=mesh,
        in_specs=(P("dp", "mp"), P("dp", "mp"), P("mp", None)),
        out_specs=(P("mp", None), P("dp", "mp")),
        check_vma=False,
    )
```
